32 devices in a mesh: dp: 8 (over z, x), tensor: 4 (over y, core).
Axes of the slice: x: 2, y: 2, z: 4, core: 2. Of those that a mesh axis runs over, the one named last changes fastest.
Arguments:
- inputs: bfloat16 [8192, 640], P('dp'), may hold values from -6 to 6
- cotangent: bfloat16 [8192, 640], P('dp'), may hold values from -6 to 6
- seq_lengths: int32 [3], replicated, may hold values from 1024 to 4096, as said below
- w_query: float32 [640, 1024], P('dp', 'tensor'), may hold values from -0.25 to 0.25
- w_kv: float32 [640, 512], P('dp'), may hold values from -0.25 to 0.25
- w_out: float32 [1024, 640], P('tensor', 'dp'), may hold values from -0.1875 to 0.1875
- w_gate_up: float32 [2, 640, 2048], P(None, 'dp', 'tensor'), may hold values from -0.25 to 0.25
- w_down: float32 [2048, 640], P('tensor', 'dp'), may hold values from -0.125 to 0.125
- gains: float32 [3072], P('dp'), may hold values from -0.3 to 0.6
- mom_query: float32 [640, 1024], P('dp', 'tensor'), may hold values from -160 to 160
- mom_kv: float32 [640, 512], P('dp'), may hold values from -160 to 160
- mom_out: float32 [1024, 640], P('tensor', 'dp'), may hold values from -160 to 160
- mom_gate_up: float32 [2, 640, 2048], P(None, 'dp', 'tensor'), may hold values from -160 to 160
- mom_down: float32 [2048, 640], P('tensor', 'dp'), may hold values from -160 to 160
- mom_gains: float32 [3072], P('dp'), may hold values from -160 to 160
Outputs:
- output: bfloat16 [8192, 640], P('dp')
- grad_input: float32 [8192, 640], P('dp')
- grad_query: float32 [640, 1024], P('dp', 'tensor')
- grad_kv: float32 [640, 512], P('dp')
- grad_out: float32 [1024, 640], P('tensor', 'dp')
- grad_gate_up: float32 [2, 640, 2048], P(None, 'dp', 'tensor')
- grad_down: float32 [2048, 640], P('tensor', 'dp')
- grad_gains: float32 [3072], P('dp')
- new_query: float32 [640, 1024], P('dp', 'tensor')
- new_kv: float32 [640, 512], P('dp')
- new_out: float32 [1024, 640], P('tensor', 'dp')
- new_gate_up: float32 [2, 640, 2048], P(None, 'dp', 'tensor')
- new_down: float32 [2048, 640], P('tensor', 'dp')
- new_gains: float32 [3072], P('dp')
- new_mom_query: float32 [640, 1024], P('dp', 'tensor')
- new_mom_kv: float32 [640, 512], P('dp')
- new_mom_out: float32 [1024, 640], P('tensor', 'dp')
- new_mom_gate_up: float32 [2, 640, 2048], P(None, 'dp', 'tensor')
- new_mom_down: float32 [2048, 640], P('tensor', 'dp')
- new_mom_gains: float32 [3072], P('dp')
The draws below stay inside these ranges and needn't reach their ends.
Inputs may be any that keep to these rules, and one draw needn't show every extreme that they name: `seq_lengths`: the 3 sequences lie end to end in token order and their lengths sum to 8192; exactly one is 4096 tokens long, and the shortest is exactly 1024 tokens.
All inputs are finite; a program needn't handle non-finite values.
Results may differ from the reference program's by a relative error of at most 0.024.
Values may be sent and summed in bfloat16 or wider, within the bound.
A program may use at most 128 MiB of HBM per device.

```python
import math
import jax
import jax.numpy as jnp
from jax import lax

D = 640
HEADS = 4
HD = 256
FF = 2048
WINDOW = 512
QB = 512
SEQ_MIN = 1024
SEQ_MID = 2048
SEQ_MAX = 4096
NS_ITERS = 5
TOKENS = 8192
NSEQ = 3


def draw_seq_lengths(key, part):
    key = jax.random.fold_in(key, 11)
    pair_count = (NSEQ - 1) // 2
    half_span = SEQ_MID - SEQ_MIN
    delta_key, chosen_key, shuffle_key = jax.random.split(key, 3)
    deltas = jax.random.randint(delta_key, (pair_count,), -half_span, half_span + 1)
    chosen = jax.random.randint(chosen_key, (), 0, pair_count)
    deltas = jnp.where(jnp.arange(pair_count) == chosen, half_span, deltas)
    firsts = SEQ_MID + deltas
    seconds = SEQ_MID - deltas
    longest = jnp.full((1,), SEQ_MAX, jnp.int32)
    lengths = jnp.concatenate([firsts.astype(jnp.int32), seconds.astype(jnp.int32), longest]).astype(jnp.int32)
    shuffle = jax.random.permutation(shuffle_key, NSEQ)
    return lengths[shuffle].astype(jnp.int32)


def block_scale(key, shape, cuts, least, largest):
    def one(dim, shards_of):
        heights = jax.random.uniform(jax.random.fold_in(jax.random.fold_in(key, 6), dim), (shards_of,), jnp.float32, least / len(cuts), largest / len(cuts))
        return jnp.repeat(jnp.exp(heights), shape[dim] // shards_of).reshape((-1,) + (1,) * (len(shape) - dim - 1))

    gain = one(*cuts[0])
    for cut in cuts[1:]:
        gain = gain * one(*cut)
    return gain


def gaussian(rng, extent, spread, limit, pieces=(), kind=jnp.bfloat16):
    loudness = block_scale(rng, extent, pieces, -0.22, 0.18) if pieces else 1.0
    values = jax.random.normal(rng, extent, jnp.float32) * spread * loudness
    return jnp.minimum(jnp.maximum(values, -limit), limit).astype(kind)


def setup_inputs(seed: int = 0) -> dict:
    streams_of = jax.random.split(jax.random.key(seed), 16)
    return {
        "inputs": gaussian(streams_of[0], (TOKENS, D), 1.0, 6.0, ((0, 8),)),
        "cotangent": gaussian(streams_of[1], (TOKENS, D), 1.0, 6.0, ((0, 8),)),
        "seq_lengths": draw_seq_lengths(jax.random.fold_in(streams_of[15], 71), 0),
        "w_query": gaussian(streams_of[3], (D, HEADS * HD), D ** -0.5, 0.25, ((0, 8), (1, 4)), jnp.float32),
        "w_kv": gaussian(streams_of[4], (D, 2 * HD), D ** -0.5, 0.25, ((0, 8),), jnp.float32),
        "w_out": gaussian(streams_of[5], (HEADS * HD, D), (HEADS * HD) ** -0.5, 0.1875, ((0, 4), (1, 8)), jnp.float32),
        "w_gate_up": gaussian(streams_of[6], (2, D, FF), D ** -0.5, 0.25, ((1, 8), (2, 4)), jnp.float32),
        "w_down": gaussian(streams_of[7], (FF, D), FF ** -0.5, 0.125, ((0, 4), (1, 8)), jnp.float32),
        "gains": jnp.clip(-0.3 + 0.90000004 * jax.random.uniform(streams_of[8], (4 * D + 2 * HD,), jnp.float32) ** block_scale(streams_of[8], (4 * D + 2 * HD,), ((0, 8),), -0.2, 0.2), -0.3, 0.6),
        "mom_query": gaussian(streams_of[9], (D, HEADS * HD), (0.3 * TOKENS ** 0.5), 160.0, ((0, 8), (1, 4)), jnp.float32),
        "mom_kv": gaussian(streams_of[10], (D, 2 * HD), (0.3 * TOKENS ** 0.5), 160.0, ((0, 8),), jnp.float32),
        "mom_out": gaussian(streams_of[11], (HEADS * HD, D), (0.3 * TOKENS ** 0.5), 160.0, ((0, 4), (1, 8)), jnp.float32),
        "mom_gate_up": gaussian(streams_of[12], (2, D, FF), (0.3 * TOKENS ** 0.5), 160.0, ((1, 8), (2, 4)), jnp.float32),
        "mom_down": gaussian(streams_of[13], (FF, D), (0.3 * TOKENS ** 0.5), 160.0, ((0, 4), (1, 8)), jnp.float32),
        "mom_gains": gaussian(streams_of[14], (4 * D + 2 * HD,), (0.3 * TOKENS ** 0.5), 160.0, ((0, 8),), jnp.float32),
    }


EPSILON = 1e-06
MOMENTUM = 0.95
MUON_RATE = 0.5
ROPE_BASE = 10000.0
COEF_FIRST = 3.4445
COEF_SECOND = -4.775
COEF_THIRD = 2.0315
MASKED = -1e+30
HIGHEST = lax.Precision.HIGHEST

@jax.custom_vjp
def low(v):
    return lax.optimization_barrier(v.astype(jnp.bfloat16)).astype(jnp.float32)

@jax.custom_vjp
def low_back(v):
    return v

def low_keep(v):
    return (low(v), None)

def low_pass(kept, grad):
    return (grad,)

def back_keep(v):
    return (v, None)

def back_low(kept, grad):
    return (low(grad),)
low.defvjp(low_keep, low_pass)
low_back.defvjp(back_keep, back_low)

def rms_scale(values, scale_gain):
    inverse = lax.rsqrt(lax.optimization_barrier(jnp.mean(values * values, axis=-1, keepdims=True)) + EPSILON)
    return values * inverse * (1.0 + scale_gain)

def rotate(values, position):
    half_dim = values.shape[-1] // 2
    exponent = jnp.arange(half_dim).astype(jnp.float32) * (-2.0 / values.shape[-1])
    frequency = jnp.power(ROPE_BASE, exponent)
    angles = position.astype(jnp.float32)[:, None] * frequency[None, :]
    cosine = jnp.cos(angles)
    sine_vals = jnp.sin(angles)
    if values.ndim == 3:
        cosine = cosine[:, None, :]
        sine_vals = sine_vals[:, None, :]
    first_half = values[..., :half_dim]
    second_half = values[..., half_dim:]
    return jnp.concatenate([first_half * cosine - second_half * sine_vals, second_half * cosine + first_half * sine_vals], axis=-1)

def orthogonalize(matrix):
    row_count, col_count = matrix.shape
    flipped = row_count > col_count
    current = matrix.T if flipped else matrix
    current = current / (jnp.sqrt(jnp.sum(current * current)) + 1e-07)
    for sweep_index in range(NS_ITERS):
        square = jnp.dot(current, current.T, precision=HIGHEST)
        polynomial = COEF_SECOND * square + COEF_THIRD * jnp.dot(square, square, precision=HIGHEST)
        current = COEF_FIRST * current + jnp.dot(polynomial, current, precision=HIGHEST)
    result = current.T if flipped else current
    return result * (MUON_RATE * math.sqrt(max(1.0, row_count / col_count)))

def attend(queries, key_rows, value_rows, segment):
    total_rows = queries.shape[0]
    head_count = queries.shape[1]
    head_dim = queries.shape[2]
    score_scale = head_dim ** (-0.5)
    pad_keys = jnp.concatenate([jnp.zeros((WINDOW, head_dim), jnp.float32), key_rows], axis=0)
    pad_values = jnp.concatenate([jnp.zeros((WINDOW, head_dim), jnp.float32), value_rows], axis=0)
    pad_segment = jnp.concatenate([jnp.full((WINDOW,), -1, jnp.int32), segment.astype(jnp.int32)])
    place_gap = jnp.arange(QB, dtype=jnp.int32)[:, None] + WINDOW - jnp.arange(QB + WINDOW, dtype=jnp.int32)[None, :]

    def block_fn(block_index):
        start = (block_index * QB).astype(jnp.int32)
        query_block = lax.dynamic_slice_in_dim(queries, start, QB, 0)
        key_block = lax.dynamic_slice_in_dim(pad_keys, start, QB + WINDOW, 0)
        value_block = lax.dynamic_slice_in_dim(pad_values, start, QB + WINDOW, 0)
        seg_query = lax.dynamic_slice_in_dim(segment.astype(jnp.int32), start, QB, 0)
        seg_key = lax.dynamic_slice_in_dim(pad_segment, start, QB + WINDOW, 0)
        allowed = (seg_query[:, None] == seg_key[None, :]) & (place_gap >= 0) & (place_gap < WINDOW)
        scores = jnp.einsum('qhd,kd->hqk', query_block, key_block, precision=HIGHEST) * score_scale
        scores = low_back(scores)
        scores = jnp.where(allowed[None], scores, MASKED)
        row_max = lax.optimization_barrier(jnp.max(scores, axis=2, keepdims=True))
        weights = jnp.exp(scores - row_max)
        attn_probs = weights / lax.optimization_barrier(jnp.sum(weights, axis=2, keepdims=True))
        return jnp.einsum('hqk,kd->qhd', low(attn_probs), value_block, precision=HIGHEST)
    blocks = lax.map(jax.checkpoint(block_fn), jnp.arange(total_rows // QB, dtype=jnp.int32))
    return blocks.reshape(total_rows, head_count, head_dim)

def reference(inputs, cotangent, seq_lengths, w_query, w_kv, w_out, w_gate_up, w_down, gains, mom_query, mom_kv, mom_out, mom_gate_up, mom_down, mom_gains):
    places = jnp.arange(TOKENS, dtype=jnp.int32)
    seq_ends = jnp.cumsum(seq_lengths).astype(jnp.int32)
    passed = places[:, None] >= seq_ends[None, :]
    segment = lax.optimization_barrier(jnp.sum(passed.astype(jnp.int32), axis=1)).astype(jnp.int32)
    seq_starts = lax.optimization_barrier(jnp.sum(jnp.where(passed, seq_lengths[None, :], 0), axis=1)).astype(jnp.int32)
    position = places - seq_starts

    def forward(input_vals, query_w, kv_w, out_w, gate_up_w, down_w, gain_all):
        gain_vals = low(gain_all)
        gain_in = gain_vals[0:D]
        gain_attn = gain_vals[D:2 * D]
        gain_pre = gain_vals[2 * D:3 * D]
        gain_post = gain_vals[3 * D:4 * D]
        gain_query = gain_vals[4 * D:4 * D + HD]
        gain_key = gain_vals[4 * D + HD:]
        normed = low(rms_scale(input_vals, gain_in))
        query_raw = low_back(jnp.dot(normed, low(query_w), precision=HIGHEST))
        kv_raw = low_back(jnp.dot(normed, low(kv_w), precision=HIGHEST))
        queries = low(rotate(rms_scale(query_raw.reshape(TOKENS, HEADS, HD), gain_query), position))
        key_rows = low(rotate(rms_scale(kv_raw[:, :HD], gain_key), position))
        value_rows = low(kv_raw[:, HD:])
        attended = attend(queries, key_rows, value_rows, segment)
        attended = low(low_back(attended.reshape(TOKENS, HEADS * HD)))
        attn_raw = low_back(jnp.dot(attended, low(out_w), precision=HIGHEST))
        hidden = input_vals + rms_scale(attn_raw, gain_attn)
        ffn_in = low(rms_scale(hidden, gain_pre))
        gate_up_low = low(gate_up_w)
        gate = low_back(jnp.dot(ffn_in, gate_up_low[0], precision=HIGHEST))
        upper = low_back(jnp.dot(ffn_in, gate_up_low[1], precision=HIGHEST))
        mixed = low(jax.nn.gelu(gate, approximate=True) * upper)
        down_raw = low_back(jnp.dot(mixed, low(down_w), precision=HIGHEST))
        return hidden + rms_scale(down_raw, gain_post)
    output_f, pullback = jax.vjp(forward, inputs.astype(jnp.float32), w_query, w_kv, w_out, w_gate_up, w_down, gains)
    grad_input, grad_query, grad_kv, grad_out, grad_gate_up, grad_down, grad_gains = pullback(cotangent.astype(jnp.float32))

    def renew(moment, gradient):
        new_moment = MOMENTUM * moment + gradient
        return (new_moment, gradient + MOMENTUM * new_moment)
    new_mom_query, nest_query = renew(mom_query, grad_query)
    new_mom_kv, nest_kv = renew(mom_kv, grad_kv)
    new_mom_out, nest_out = renew(mom_out, grad_out)
    new_mom_gate_up, nest_gate_up = renew(mom_gate_up, grad_gate_up)
    new_mom_down, nest_down = renew(mom_down, grad_down)
    new_mom_gains, nest_gains = renew(mom_gains, grad_gains)
    quarter = FF // HEADS
    new_query = w_query - jnp.concatenate([orthogonalize(nest_query[:, head_index * HD:(head_index + 1) * HD]) for head_index in range(HEADS)], axis=1)
    new_kv = w_kv - jnp.concatenate([orthogonalize(nest_kv[:, :HD]), orthogonalize(nest_kv[:, HD:])], axis=1)
    new_out = w_out - jnp.concatenate([orthogonalize(nest_out[head_index * HD:(head_index + 1) * HD]) for head_index in range(HEADS)], axis=0)
    new_gate_up = w_gate_up - jnp.stack([jnp.concatenate([orthogonalize(nest_gate_up[half_index][:, block_index * quarter:(block_index + 1) * quarter]) for block_index in range(HEADS)], axis=1) for half_index in range(2)], axis=0)
    new_down = w_down - jnp.concatenate([orthogonalize(nest_down[block_index * quarter:(block_index + 1) * quarter]) for block_index in range(HEADS)], axis=0)
    new_gains = gains - 0.1 / math.sqrt(TOKENS) * nest_gains
    return (output_f.astype(jnp.bfloat16), grad_input, grad_query, grad_kv, grad_out, grad_gate_up, grad_down, grad_gains, new_query, new_kv, new_out, new_gate_up, new_down, new_gains, new_mom_query, new_mom_kv, new_mom_out, new_mom_gate_up, new_mom_down, new_mom_gains)
```

```python
import math

import jax
import jax.numpy as jnp
from jax import lax
from jax.experimental import pallas as pl
from jax.experimental.pallas import tpu as pltpu
from jax.sharding import PartitionSpec as P

WINDOW = 512
NS_ITERS = 5


EPSILON = 1e-06
MOMENTUM = 0.95
MUON_RATE = 0.5
ROPE_BASE = 10000.0
COEF_FIRST = 3.4445
COEF_SECOND = -4.775
COEF_THIRD = 2.0315
MASKED = -1e30
LANES = 128


def from_behind(block, axis, distance):
    devices = range(lax.axis_size(axis))
    route = [(i - distance, i) for i in devices if i - distance in devices]
    return lax.ppermute(block, axis, route)


def rms_scale(values, scale_gain):
    inverse = lax.rsqrt(jnp.mean(values * values, axis=-1, keepdims=True) + EPSILON)
    return values * inverse * (1.0 + scale_gain)


def rotate(values, position):
    half_dim = values.shape[-1] // 2
    exponent = jnp.arange(half_dim).astype(jnp.float32) * (-2.0 / values.shape[-1])
    frequency = jnp.power(ROPE_BASE, exponent)
    angles = position.astype(jnp.float32)[:, None] * frequency[None, :]
    cosine = jnp.cos(angles)
    sine_vals = jnp.sin(angles)
    first_half = values[..., :half_dim]
    second_half = values[..., half_dim:]
    return jnp.concatenate(
        [
            first_half * cosine - second_half * sine_vals,
            second_half * cosine + first_half * sine_vals,
        ],
        axis=-1,
    )


def sweep_kernel(start_ref, block_ref, result_ref):
    low_type = jnp.bfloat16
    full_type = jnp.float32

    def halves(values):
        high = values.astype(low_type)
        return high, (values - high.astype(full_type)).astype(low_type)

    def product(left, right):
        left_high, left_low = left
        right_high, right_low = right
        total = jnp.dot(left_high, right_high, preferred_element_type=full_type)
        total += jnp.dot(left_high, right_low, preferred_element_type=full_type)
        return total + jnp.dot(left_low, right_high, preferred_element_type=full_type)

    result_ref[...] = start_ref[...]

    @pl.loop(0, NS_ITERS)
    def _(sweep_index):
        current = result_ref[...]
        current_halves = halves(current)
        square = block_ref[...] * lax.dot_general(
            current_halves[0],
            current_halves[0],
            (((1,), (1,)), ((), ())),
            preferred_element_type=full_type,
        )
        square_halves = halves(square)
        polynomial = COEF_SECOND * square + COEF_THIRD * product(square_halves, square_halves)
        result_ref[...] = COEF_FIRST * current + product(halves(polynomial), current_halves)


def orthogonalize(matrix, paired):
    rows = matrix.shape[0]
    half = rows // 2
    row_sums = jnp.sum(matrix * matrix, axis=1)
    upper, lower = jnp.sum(row_sums[:half]), jnp.sum(row_sums[half:])
    own_half = jnp.arange(rows) < half
    sums = jnp.where(paired, jnp.where(own_half, upper, lower), upper + lower)
    start = matrix / (jnp.sqrt(sums) + 1e-07)[:, None]
    same = own_half[:, None] == own_half[None, :]
    block = jnp.where(paired, same.astype(jnp.float32), 1.0)
    return pl.pallas_call(
        sweep_kernel,
        out_shape=jax.ShapeDtypeStruct(matrix.shape, jnp.float32),
        in_specs=[pl.BlockSpec(memory_space=pltpu.VMEM)] * 2,
        out_specs=pl.BlockSpec(memory_space=pltpu.VMEM),
        compiler_params=pltpu.CompilerParams(vmem_limit_bytes=40 * 1024 * 1024),
    )(start, block)


def shards(
    inputs,
    cotangent,
    seq_lengths,
    w_query,
    w_kv,
    w_out,
    w_gate_up,
    w_down,
    gains,
    mom_query,
    mom_kv,
    mom_out,
    mom_gate_up,
    mom_down,
    mom_gains,
):
    low_type = jnp.bfloat16
    full_type = jnp.float32
    row_count, width = inputs.shape
    head_dim = w_kv.shape[1] // 2
    hidden = w_down.shape[0]
    shard_rows = w_query.shape[0]
    dp_count = lax.axis_size("dp")
    dp_index = lax.axis_index("dp")
    tensor_count = lax.axis_size("tensor")
    tensor_index = lax.axis_index("tensor")
    own_rows = row_count // tensor_count
    window_rows = own_rows + WINDOW
    quarter = 2 * head_dim // tensor_count
    gain_size = gains.shape[0]
    gain_rows = -(-gain_size // LANES)
    score_scale = head_dim ** (-0.5)
    task_width = hidden
    matrix_width = 4 * task_width
    both = ("tensor", "dp")

    def ein(form, left, right):
        return jnp.einsum(form, left, right, preferred_element_type=full_type)

    def pack_gains(values):
        padded = jnp.pad(values, (0, gain_rows * LANES - gain_size)).reshape(gain_rows, LANES)
        return jnp.pad(padded, ((0, shard_rows - gain_rows), (0, 0)))

    halo = from_behind(inputs[row_count - WINDOW :], "dp", 1)
    kv_quarter = lax.dynamic_slice_in_dim(w_kv, tensor_index * quarter, quarter, 1)
    packed = jnp.concatenate(
        [w_query, w_out.T, w_gate_up[0], w_gate_up[1], w_down.T, kv_quarter, pack_gains(gains)],
        axis=1,
    ).astype(low_type)
    whole = lax.all_gather(packed, both, axis=0, tiled=True)
    whole = whole.reshape(tensor_count, width, packed.shape[1])
    query_weight = whole[:, :, :head_dim]
    out_weight = whole[:, :, head_dim : 2 * head_dim]
    gate_weight = whole[:, :, task_width : 2 * task_width]
    up_weight = whole[:, :, 2 * task_width : 3 * task_width]
    down_weight = whole[:, :, 3 * task_width : matrix_width]
    kv_weight = whole[:, :, matrix_width : matrix_width + quarter]
    kv_weight = kv_weight.transpose(1, 0, 2).reshape(width, 2 * head_dim)
    gain_vals = whole[0, :, matrix_width + quarter :].reshape(dp_count, shard_rows * LANES)
    gain_vals = gain_vals[:, :gain_size].reshape(-1).astype(full_type)
    gain_in = gain_vals[0:width]
    gain_attn = gain_vals[width : 2 * width]
    gain_pre = gain_vals[2 * width : 3 * width]
    gain_post = gain_vals[3 * width : 4 * width]
    gain_query = gain_vals[4 * width : 4 * width + head_dim]
    gain_key = gain_vals[4 * width + head_dim :]

    first_row = tensor_index * own_rows
    places = dp_index * row_count + first_row - WINDOW
    places = places + jnp.arange(window_rows, dtype=jnp.int32)
    seq_ends = jnp.cumsum(seq_lengths)
    passed = places[:, None] >= seq_ends[None, :]
    segment = jnp.sum(passed.astype(jnp.int32), axis=1)
    seq_starts = jnp.sum(jnp.where(passed, seq_lengths[None, :], 0), axis=1)
    segment = jnp.where(places < 0, -1, segment)
    position = places - seq_starts
    gap = places[WINDOW:, None] - places[None, :]
    allowed = (segment[WINDOW:, None] == segment[None, :]) & (gap >= 0) & (gap < WINDOW)
    allowed = jnp.broadcast_to(allowed[None], (tensor_count, own_rows, window_rows))
    allowed = allowed.reshape(tensor_count * own_rows, window_rows)

    def query_map(raw, scale_gain):
        flat = raw.reshape(tensor_count * own_rows, head_dim)
        return rotate(rms_scale(flat, scale_gain), jnp.tile(position[WINDOW:], tensor_count))

    def key_map(raw, scale_gain):
        return rotate(rms_scale(raw, scale_gain), position)

    def activate(gate_raw, up_raw):
        return jax.nn.gelu(gate_raw, approximate=True) * up_raw

    extended = jnp.concatenate([halo, inputs], axis=0)
    window_in = lax.dynamic_slice_in_dim(extended, first_row, window_rows, 0).astype(full_type)
    own_in = window_in[WINDOW:]
    back_out = lax.dynamic_slice_in_dim(cotangent, first_row, own_rows, 0).astype(full_type)
    normed_f, input_norm_back = jax.vjp(rms_scale, window_in, gain_in)
    normed_window = normed_f.astype(low_type)
    normed = normed_window[WINDOW:]
    query_raw = ein("td,hdc->htc", normed, query_weight)
    kv_raw = ein("td,dc->tc", normed_window, kv_weight)
    queries_f, query_back = jax.vjp(query_map, query_raw, gain_query)
    keys_f, key_back = jax.vjp(key_map, kv_raw[:, :head_dim], gain_key)
    queries = queries_f.astype(low_type)
    key_rows = keys_f.astype(low_type)
    value_rows = kv_raw[:, head_dim:].astype(low_type)
    scores = ein("qd,kd->qk", queries, key_rows) * score_scale
    scores = jnp.where(allowed, scores, MASKED)
    weights = jnp.exp(scores - jnp.max(scores, axis=1, keepdims=True))
    probs = weights / jnp.sum(weights, axis=1, keepdims=True)
    probs_low = probs.astype(low_type)
    attended = ein("qk,kd->qd", probs_low, value_rows).astype(low_type)
    attended = attended.reshape(tensor_count, own_rows, head_dim)
    attn_raw = ein("htc,hdc->td", attended, out_weight)
    branch_attn, attn_norm_back = jax.vjp(rms_scale, attn_raw, gain_attn)
    hidden_rows = own_in + branch_attn
    ffn_f, pre_norm_back = jax.vjp(rms_scale, hidden_rows, gain_pre)
    ffn_in = ffn_f.astype(low_type)
    gate = ein("td,hdf->htf", ffn_in, gate_weight)
    up = ein("td,hdf->htf", ffn_in, up_weight)
    mixed_f, activate_back = jax.vjp(activate, gate, up)
    mixed = mixed_f.astype(low_type)
    down_raw = ein("htf,hdf->td", mixed, down_weight)
    branch_ffn, post_norm_back = jax.vjp(rms_scale, down_raw, gain_post)
    output_own = (hidden_rows + branch_ffn).astype(low_type)
    output = lax.all_gather(output_own, "tensor", axis=0, tiled=True)

    back_down_f, grad_gain_post = post_norm_back(back_out)
    back_down = back_down_f.astype(low_type)
    grad_down = ein("td,htf->hdf", back_down, mixed)
    back_gate_f, back_up_f = activate_back(ein("td,hdf->htf", back_down, down_weight))
    back_gate = back_gate_f.astype(low_type)
    back_up = back_up_f.astype(low_type)
    grad_gate = ein("td,htf->hdf", ffn_in, back_gate)
    grad_up = ein("td,htf->hdf", ffn_in, back_up)
    back_ffn = ein("htf,hdf->td", back_gate, gate_weight) + ein(
        "htf,hdf->td", back_up, up_weight
    )
    back_pre, grad_gain_pre = pre_norm_back(back_ffn)
    back_hidden = back_out + back_pre
    back_attn_f, grad_gain_attn = attn_norm_back(back_hidden)
    back_attn = back_attn_f.astype(low_type)
    grad_out = ein("td,htc->hdc", back_attn, attended)
    back_attended = ein("td,hdc->htc", back_attn, out_weight).astype(low_type)
    back_attended = back_attended.reshape(tensor_count * own_rows, head_dim)
    back_probs = ein("qd,kd->qk", back_attended, value_rows)
    row_dot = jnp.sum(probs * back_probs, axis=1, keepdims=True)
    back_scores = (probs * (back_probs - row_dot)).astype(low_type)
    back_queries = ein("qk,kd->qd", back_scores, key_rows) * score_scale
    back_keys = ein("qk,qd->kd", back_scores, queries) * score_scale
    back_values = ein("qk,qd->kd", probs_low, back_attended)
    back_query_raw_f, grad_gain_query = query_back(back_queries)
    back_query_raw = back_query_raw_f.astype(low_type)
    back_key_raw, grad_gain_key = key_back(back_keys)
    back_kv = jnp.concatenate([back_key_raw, back_values], axis=1).astype(low_type)
    grad_query = ein("td,htc->hdc", normed, back_query_raw)
    grad_kv = ein("td,tc->dc", normed_window, back_kv)
    back_normed = ein("tc,dc->td", back_kv, kv_weight)
    back_normed = back_normed.at[WINDOW:].add(ein("htc,hdc->td", back_query_raw, query_weight))
    back_in, grad_gain_in = input_norm_back(back_normed)

    grad_gains = jnp.concatenate(
        [grad_gain_in, grad_gain_attn, grad_gain_pre, grad_gain_post, grad_gain_query, grad_gain_key]
    )
    gain_block = jax.vmap(pack_gains)(grad_gains.reshape(dp_count, gain_size))
    gain_block = gain_block.reshape(1, width, LANES) * (1.0 / tensor_count)
    gain_block = jnp.broadcast_to(gain_block, (tensor_count, width, LANES))
    kv_parts = grad_kv.reshape(width, tensor_count, quarter).transpose(1, 0, 2)
    grads = jnp.concatenate(
        [grad_query, grad_out, grad_gate, grad_up, grad_down, kv_parts, gain_block], axis=2
    ).astype(low_type)
    summed = lax.psum_scatter(
        grads.reshape(tensor_count * width, grads.shape[2]), both, scatter_dimension=0, tiled=True
    ).astype(full_type)
    shared = lax.all_gather(summed[:, matrix_width:], "tensor", axis=0)
    grad_query = summed[:, :head_dim]
    grad_out = summed[:, head_dim : 2 * head_dim].T
    grad_gate_up = jnp.stack(
        [summed[:, task_width : 2 * task_width], summed[:, 2 * task_width : 3 * task_width]]
    )
    grad_down = summed[:, 3 * task_width : matrix_width].T
    grad_kv = shared[:, :, :quarter].transpose(1, 0, 2).reshape(shard_rows, 2 * head_dim)
    grad_gains = jnp.sum(shared[:, :gain_rows, quarter:], axis=0).reshape(-1)[:gain_size]

    spread = jnp.zeros((row_count + WINDOW, width), full_type)
    spread = lax.dynamic_update_slice_in_dim(
        spread, back_in.at[WINDOW:].add(back_hidden), first_row, 0
    )
    spread = lax.psum(spread.astype(low_type), "tensor")
    behind = from_behind(spread[:WINDOW], "dp", -1).astype(full_type)
    grad_input = spread[WINDOW:].astype(full_type).at[row_count - WINDOW :].add(behind)

    new_mom_query = MOMENTUM * mom_query + grad_query
    new_mom_kv = MOMENTUM * mom_kv + grad_kv
    new_mom_out = MOMENTUM * mom_out + grad_out
    new_mom_gate_up = MOMENTUM * mom_gate_up + grad_gate_up
    new_mom_down = MOMENTUM * mom_down + grad_down
    new_mom_gains = MOMENTUM * mom_gains + grad_gains
    nest_query = grad_query + MOMENTUM * new_mom_query
    nest_kv = grad_kv + MOMENTUM * new_mom_kv
    nest_out = grad_out + MOMENTUM * new_mom_out
    nest_gate_up = grad_gate_up + MOMENTUM * new_mom_gate_up
    nest_down = grad_down + MOMENTUM * new_mom_down
    nest_gains = grad_gains + MOMENTUM * new_mom_gains
    new_gains = gains - 0.1 / math.sqrt(row_count * dp_count) * nest_gains
    tasks = jnp.stack(
        [
            jnp.concatenate([nest_query, nest_out.T], axis=1),
            nest_gate_up[0],
            nest_gate_up[1],
            nest_down.T,
            nest_kv,
        ]
    ).astype(low_type)
    task_count = tasks.shape[0]
    tasks = jnp.pad(tasks, ((0, dp_count - task_count), (0, 0), (0, 0)))
    mine = lax.all_to_all(tasks, "dp", split_axis=0, concat_axis=0, tiled=True)
    mine = mine.reshape(width, task_width).T.astype(full_type)
    paired = (dp_index == 0) | (dp_index == 4)
    steps = orthogonalize(mine, paired).T.astype(low_type).reshape(dp_count, shard_rows, task_width)
    steps = lax.all_to_all(steps, "dp", split_axis=0, concat_axis=0, tiled=True)
    steps = steps.astype(full_type)

    def rate(rows, columns):
        return MUON_RATE * math.sqrt(max(1.0, rows / columns))

    new_query = w_query - rate(width, head_dim) * steps[0][:, :head_dim]
    new_out = w_out - rate(head_dim, width) * steps[0][:, head_dim:].T
    new_gate_up = w_gate_up - rate(width, hidden) * steps[1:3]
    new_down = w_down - rate(hidden, width) * steps[3].T
    new_kv = w_kv - rate(width, head_dim) * steps[4]
    return (
        output,
        grad_input,
        grad_query,
        grad_kv,
        grad_out,
        grad_gate_up,
        grad_down,
        grad_gains,
        new_query,
        new_kv,
        new_out,
        new_gate_up,
        new_down,
        new_gains,
        new_mom_query,
        new_mom_kv,
        new_mom_out,
        new_mom_gate_up,
        new_mom_down,
        new_mom_gains,
    )


def solution(mesh):
    return jax.shard_map(
        shards,
        mesh=mesh,
        in_specs=(
            P("dp", None),
            P("dp", None),
            P(),
            P("dp", "tensor"),
            P("dp", None),
            P("tensor", "dp"),
            P(None, "dp", "tensor"),
            P("tensor", "dp"),
            P("dp"),
            P("dp", "tensor"),
            P("dp", None),
            P("tensor", "dp"),
            P(None, "dp", "tensor"),
            P("tensor", "dp"),
            P("dp"),
        ),
        out_specs=(
            P("dp", None),
            P("dp", None),
            P("dp", "tensor"),
            P("dp", None),
            P("tensor", "dp"),
            P(None, "dp", "tensor"),
            P("tensor", "dp"),
            P("dp"),
            P("dp", "tensor"),
            P("dp", None),
            P("tensor", "dp"),
            P(None, "dp", "tensor"),
            P("tensor", "dp"),
            P("dp"),
            P("dp", "tensor"),
            P("dp", None),
            P("tensor", "dp"),
            P(None, "dp", "tensor"),
            P("tensor", "dp"),
            P("dp"),
        ),
        check_vma=False,
    )
```

```python
import functools
import math

import jax
import jax.numpy as jnp
from jax import lax
from jax.experimental import pallas as pl
from jax.experimental.pallas import tpu as pltpu
from jax.sharding import PartitionSpec as P

WINDOW = 512
NS_ITERS = 5


EPSILON = 1e-06
MOMENTUM = 0.95
MUON_RATE = 0.5
ROPE_BASE = 10000.0
COEF_FIRST = 3.4445
COEF_SECOND = -4.775
COEF_THIRD = 2.0315
MASKED = -1e30
LANES = 128


def from_behind(block, axis, distance):
    devices = range(lax.axis_size(axis))
    route = [(i - distance, i) for i in devices if i - distance in devices]
    return lax.ppermute(block, axis, route)


def rms_scale(values, scale_gain):
    inverse = lax.rsqrt(jnp.mean(values * values, axis=-1, keepdims=True) + EPSILON)
    return values * inverse * (1.0 + scale_gain)


def rotate(values, position):
    half_dim = values.shape[-1] // 2
    exponent = jnp.arange(half_dim).astype(jnp.float32) * (-2.0 / values.shape[-1])
    frequency = jnp.power(ROPE_BASE, exponent)
    angles = position.astype(jnp.float32)[:, None] * frequency[None, :]
    cosine = jnp.cos(angles)
    sine_vals = jnp.sin(angles)
    first_half = values[..., :half_dim]
    second_half = values[..., half_dim:]
    return jnp.concatenate(
        [
            first_half * cosine - second_half * sine_vals,
            second_half * cosine + first_half * sine_vals,
        ],
        axis=-1,
    )


def sweep_kernel(start_ref, block_ref, result_ref):
    low_type = jnp.bfloat16
    full_type = jnp.float32

    def halves(values):
        high = values.astype(low_type)
        return high, (values - high.astype(full_type)).astype(low_type)

    def product(left, right):
        left_high, left_low = left
        right_high, right_low = right
        total = jnp.dot(left_high, right_high, preferred_element_type=full_type)
        total += jnp.dot(left_high, right_low, preferred_element_type=full_type)
        return total + jnp.dot(left_low, right_high, preferred_element_type=full_type)

    result_ref[...] = start_ref[...]

    @pl.loop(0, NS_ITERS)
    def _(sweep_index):
        current = result_ref[...]
        current_halves = halves(current)
        square = block_ref[...] * lax.dot_general(
            current_halves[0],
            current_halves[0],
            (((1,), (1,)), ((), ())),
            preferred_element_type=full_type,
        )
        square_halves = halves(square)
        polynomial = COEF_SECOND * square + COEF_THIRD * product(square_halves, square_halves)
        result_ref[...] = COEF_FIRST * current + product(halves(polynomial), current_halves)


def orthogonalize(matrix, paired):
    rows = matrix.shape[0]
    half = rows // 2
    row_sums = jnp.sum(matrix * matrix, axis=1)
    upper, lower = jnp.sum(row_sums[:half]), jnp.sum(row_sums[half:])
    own_half = jnp.arange(rows) < half
    sums = jnp.where(paired, jnp.where(own_half, upper, lower), upper + lower)
    start = matrix / (jnp.sqrt(sums) + 1e-07)[:, None]
    same = own_half[:, None] == own_half[None, :]
    block = jnp.where(paired, same.astype(jnp.float32), 1.0)
    return pl.pallas_call(
        sweep_kernel,
        out_shape=jax.ShapeDtypeStruct(matrix.shape, jnp.float32),
        in_specs=[pl.BlockSpec(memory_space=pltpu.VMEM)] * 2,
        out_specs=pl.BlockSpec(memory_space=pltpu.VMEM),
        compiler_params=pltpu.CompilerParams(vmem_limit_bytes=40 * 1024 * 1024),
    )(start, block)


def gradient_kernel(
    head_dim,
    normed_ref,
    back_attn_ref,
    ffn_in_ref,
    back_down_ref,
    back_query_ref,
    attended_ref,
    back_gate_ref,
    back_up_ref,
    mixed_ref,
    back_kv_ref,
    gain_ref,
    grads_ref,
):
    def put(start, left, right):
        product = jnp.dot(left, right, preferred_element_type=jnp.float32)
        grads_ref[0, :, start : start + right.shape[1]] = product.astype(grads_ref.dtype)

    hidden = mixed_ref.shape[2]
    matrix_width = 2 * head_dim + 3 * hidden
    put(0, normed_ref[:, WINDOW:], back_query_ref[0])
    put(head_dim, back_attn_ref[...], attended_ref[0])
    put(2 * head_dim, ffn_in_ref[...], back_gate_ref[0])
    put(2 * head_dim + hidden, ffn_in_ref[...], back_up_ref[0])
    put(2 * head_dim + 2 * hidden, back_down_ref[...], mixed_ref[0])
    put(matrix_width, normed_ref[...], back_kv_ref[...])
    grads_ref[0, :, matrix_width + back_kv_ref.shape[1] :] = gain_ref[...]


def packed_gradients(lefts, rights, back_kv, gain_block, head_dim):
    heads = rights[0].shape[0]
    width = lefts[0].shape[0]
    quarter = back_kv.shape[1] // heads
    columns = sum(right.shape[2] for right in rights) + quarter + LANES
    whole = [pl.BlockSpec(left.shape, lambda h: (0, 0)) for left in lefts]
    by_head = [pl.BlockSpec((1,) + right.shape[1:], lambda h: (h, 0, 0)) for right in rights]
    return pl.pallas_call(
        functools.partial(gradient_kernel, head_dim),
        grid=(heads,),
        out_shape=jax.ShapeDtypeStruct((heads, width, columns), jnp.bfloat16),
        in_specs=whole
        + by_head
        + [
            pl.BlockSpec((back_kv.shape[0], quarter), lambda h: (0, h)),
            pl.BlockSpec(gain_block.shape, lambda h: (0, 0)),
        ],
        out_specs=pl.BlockSpec((1, width, columns), lambda h: (h, 0, 0)),
        compiler_params=pltpu.CompilerParams(vmem_limit_bytes=40 * 1024 * 1024),
    )(*lefts, *rights, back_kv, gain_block)


def shards(
    inputs,
    cotangent,
    seq_lengths,
    w_query,
    w_kv,
    w_out,
    w_gate_up,
    w_down,
    gains,
    mom_query,
    mom_kv,
    mom_out,
    mom_gate_up,
    mom_down,
    mom_gains,
):
    low_type = jnp.bfloat16
    full_type = jnp.float32
    row_count, width = inputs.shape
    head_dim = w_kv.shape[1] // 2
    hidden = w_down.shape[0]
    shard_rows = w_query.shape[0]
    dp_count = lax.axis_size("dp")
    dp_index = lax.axis_index("dp")
    tensor_count = lax.axis_size("tensor")
    tensor_index = lax.axis_index("tensor")
    own_rows = row_count // tensor_count
    window_rows = own_rows + WINDOW
    quarter = 2 * head_dim // tensor_count
    gain_size = gains.shape[0]
    gain_rows = -(-gain_size // LANES)
    score_scale = head_dim ** (-0.5)
    task_width = hidden
    matrix_width = 4 * task_width
    both = ("tensor", "dp")

    def ein(form, left, right):
        return jnp.einsum(form, left, right, preferred_element_type=full_type)

    def pack_gains(values):
        padded = jnp.pad(values, (0, gain_rows * LANES - gain_size)).reshape(gain_rows, LANES)
        return jnp.pad(padded, ((0, shard_rows - gain_rows), (0, 0)))

    halo = from_behind(inputs[row_count - WINDOW :], "dp", 1)
    kv_quarter = lax.dynamic_slice_in_dim(w_kv, tensor_index * quarter, quarter, 1)
    packed = jnp.concatenate(
        [w_query, w_out.T, w_gate_up[0], w_gate_up[1], w_down.T, kv_quarter, pack_gains(gains)],
        axis=1,
    ).astype(low_type)
    whole = lax.all_gather(packed, both, axis=0, tiled=True)
    whole = whole.reshape(tensor_count, width, packed.shape[1])
    query_weight = whole[:, :, :head_dim]
    out_weight = whole[:, :, head_dim : 2 * head_dim]
    gate_weight = whole[:, :, task_width : 2 * task_width]
    up_weight = whole[:, :, 2 * task_width : 3 * task_width]
    down_weight = whole[:, :, 3 * task_width : matrix_width]
    kv_weight = whole[:, :, matrix_width : matrix_width + quarter]
    kv_weight = kv_weight.transpose(1, 0, 2).reshape(width, 2 * head_dim)
    gain_vals = whole[0, :, matrix_width + quarter :].reshape(dp_count, shard_rows * LANES)
    gain_vals = gain_vals[:, :gain_size].reshape(-1).astype(full_type)
    gain_in = gain_vals[0:width]
    gain_attn = gain_vals[width : 2 * width]
    gain_pre = gain_vals[2 * width : 3 * width]
    gain_post = gain_vals[3 * width : 4 * width]
    gain_query = gain_vals[4 * width : 4 * width + head_dim]
    gain_key = gain_vals[4 * width + head_dim :]

    first_row = tensor_index * own_rows
    places = dp_index * row_count + first_row - WINDOW
    places = places + jnp.arange(window_rows, dtype=jnp.int32)
    seq_ends = jnp.cumsum(seq_lengths)
    passed = places[:, None] >= seq_ends[None, :]
    segment = jnp.sum(passed.astype(jnp.int32), axis=1)
    seq_starts = jnp.sum(jnp.where(passed, seq_lengths[None, :], 0), axis=1)
    segment = jnp.where(places < 0, -1, segment)
    position = places - seq_starts
    gap = places[WINDOW:, None] - places[None, :]
    allowed = (segment[WINDOW:, None] == segment[None, :]) & (gap >= 0) & (gap < WINDOW)
    allowed = jnp.broadcast_to(allowed[None], (tensor_count, own_rows, window_rows))
    allowed = allowed.reshape(tensor_count * own_rows, window_rows)

    def query_map(raw, scale_gain):
        flat = raw.reshape(tensor_count * own_rows, head_dim)
        return rotate(rms_scale(flat, scale_gain), jnp.tile(position[WINDOW:], tensor_count))

    def key_map(raw, scale_gain):
        return rotate(rms_scale(raw, scale_gain), position)

    def activate(gate_raw, up_raw):
        return jax.nn.gelu(gate_raw, approximate=True) * up_raw

    extended = jnp.concatenate([halo, inputs], axis=0)
    window_in = lax.dynamic_slice_in_dim(extended, first_row, window_rows, 0).astype(full_type)
    own_in = window_in[WINDOW:]
    back_out = lax.dynamic_slice_in_dim(cotangent, first_row, own_rows, 0).astype(full_type)
    normed_f, input_norm_back = jax.vjp(rms_scale, window_in, gain_in)
    normed_window = normed_f.astype(low_type)
    normed = normed_window[WINDOW:]
    query_raw = ein("td,hdc->htc", normed, query_weight)
    kv_raw = ein("td,dc->tc", normed_window, kv_weight)
    queries_f, query_back = jax.vjp(query_map, query_raw, gain_query)
    keys_f, key_back = jax.vjp(key_map, kv_raw[:, :head_dim], gain_key)
    queries = queries_f.astype(low_type)
    key_rows = keys_f.astype(low_type)
    value_rows = kv_raw[:, head_dim:].astype(low_type)
    scores = ein("qd,kd->qk", queries, key_rows) * score_scale
    scores = jnp.where(allowed, scores, MASKED)
    weights = jnp.exp(scores - jnp.max(scores, axis=1, keepdims=True))
    probs = weights / jnp.sum(weights, axis=1, keepdims=True)
    probs_low = probs.astype(low_type)
    attended = ein("qk,kd->qd", probs_low, value_rows).astype(low_type)
    attended = attended.reshape(tensor_count, own_rows, head_dim)
    attn_raw = ein("htc,hdc->td", attended, out_weight)
    branch_attn, attn_norm_back = jax.vjp(rms_scale, attn_raw, gain_attn)
    hidden_rows = own_in + branch_attn
    ffn_f, pre_norm_back = jax.vjp(rms_scale, hidden_rows, gain_pre)
    ffn_in = ffn_f.astype(low_type)
    gate = ein("td,hdf->htf", ffn_in, gate_weight)
    up = ein("td,hdf->htf", ffn_in, up_weight)
    mixed_f, activate_back = jax.vjp(activate, gate, up)
    mixed = mixed_f.astype(low_type)
    down_raw = ein("htf,hdf->td", mixed, down_weight)
    branch_ffn, post_norm_back = jax.vjp(rms_scale, down_raw, gain_post)
    output_own = (hidden_rows + branch_ffn).astype(low_type)

    back_down_f, grad_gain_post = post_norm_back(back_out)
    back_down = back_down_f.astype(low_type)
    back_gate_f, back_up_f = activate_back(ein("td,hdf->htf", back_down, down_weight))
    back_gate = back_gate_f.astype(low_type)
    back_up = back_up_f.astype(low_type)
    back_ffn = ein("htf,hdf->td", back_gate, gate_weight) + ein(
        "htf,hdf->td", back_up, up_weight
    )
    back_pre, grad_gain_pre = pre_norm_back(back_ffn)
    back_hidden = back_out + back_pre
    back_attn_f, grad_gain_attn = attn_norm_back(back_hidden)
    back_attn = back_attn_f.astype(low_type)
    back_attended = ein("td,hdc->htc", back_attn, out_weight).astype(low_type)
    back_attended = back_attended.reshape(tensor_count * own_rows, head_dim)
    back_probs = ein("qd,kd->qk", back_attended, value_rows)
    row_dot = jnp.sum(probs * back_probs, axis=1, keepdims=True)
    back_scores = (probs * (back_probs - row_dot)).astype(low_type)
    back_queries = ein("qk,kd->qd", back_scores, key_rows) * score_scale
    back_keys = ein("qk,qd->kd", back_scores, queries) * score_scale
    back_values = ein("qk,qd->kd", probs_low, back_attended)
    back_query_raw_f, grad_gain_query = query_back(back_queries)
    back_query_raw = back_query_raw_f.astype(low_type)
    back_key_raw, grad_gain_key = key_back(back_keys)
    back_kv = jnp.concatenate([back_key_raw, back_values], axis=1).astype(low_type)
    back_normed = ein("tc,dc->td", back_kv, kv_weight)
    back_normed = back_normed.at[WINDOW:].add(ein("htc,hdc->td", back_query_raw, query_weight))
    back_in, grad_gain_in = input_norm_back(back_normed)

    grad_gains = jnp.concatenate(
        [grad_gain_in, grad_gain_attn, grad_gain_pre, grad_gain_post, grad_gain_query, grad_gain_key]
    )
    gain_block = jax.vmap(pack_gains)(grad_gains.reshape(dp_count, gain_size))
    gain_block = gain_block.reshape(width, LANES) * (1.0 / tensor_count)
    grads = packed_gradients(
        [normed_window.T, back_attn.T, ffn_in.T, back_down.T],
        [back_query_raw, attended, back_gate, back_up, mixed],
        back_kv,
        gain_block.astype(low_type),
        head_dim,
    )
    summed = lax.psum_scatter(
        grads.reshape(tensor_count * width, grads.shape[2]), both, scatter_dimension=0, tiled=True
    ).astype(full_type)
    shared = lax.all_gather(summed[:, matrix_width:], "tensor", axis=0)
    grad_query = summed[:, :head_dim]
    grad_out = summed[:, head_dim : 2 * head_dim].T
    grad_gate_up = jnp.stack(
        [summed[:, task_width : 2 * task_width], summed[:, 2 * task_width : 3 * task_width]]
    )
    grad_down = summed[:, 3 * task_width : matrix_width].T
    grad_kv = shared[:, :, :quarter].transpose(1, 0, 2).reshape(shard_rows, 2 * head_dim)
    grad_gains = jnp.sum(shared[:, :gain_rows, quarter:], axis=0).reshape(-1)[:gain_size]

    grad_own = back_in[WINDOW:] + back_hidden
    for part in range(WINDOW // own_rows):
        rows = back_in[part * own_rows : (part + 1) * own_rows].astype(low_type)
        moved = from_behind(rows, ("dp", "tensor"), part - WINDOW // own_rows)
        grad_own = grad_own + moved.astype(full_type)
    own_pair = jnp.concatenate([output_own, grad_own.astype(low_type)], axis=1)

    new_mom_query = MOMENTUM * mom_query + grad_query
    new_mom_kv = MOMENTUM * mom_kv + grad_kv
    new_mom_out = MOMENTUM * mom_out + grad_out
    new_mom_gate_up = MOMENTUM * mom_gate_up + grad_gate_up
    new_mom_down = MOMENTUM * mom_down + grad_down
    new_mom_gains = MOMENTUM * mom_gains + grad_gains
    nest_query = grad_query + MOMENTUM * new_mom_query
    nest_kv = grad_kv + MOMENTUM * new_mom_kv
    nest_out = grad_out + MOMENTUM * new_mom_out
    nest_gate_up = grad_gate_up + MOMENTUM * new_mom_gate_up
    nest_down = grad_down + MOMENTUM * new_mom_down
    nest_gains = grad_gains + MOMENTUM * new_mom_gains
    new_gains = gains - 0.1 / math.sqrt(row_count * dp_count) * nest_gains
    tasks = jnp.stack(
        [
            jnp.concatenate([nest_query, nest_out.T], axis=1),
            nest_gate_up[0],
            nest_gate_up[1],
            nest_down.T,
            nest_kv,
        ]
    ).astype(low_type)
    task_count = tasks.shape[0]
    tasks = jnp.pad(tasks, ((0, dp_count - task_count), (0, 0), (0, 0)))
    mine = lax.all_to_all(tasks, "dp", split_axis=0, concat_axis=0, tiled=True)
    mine, own_pair = lax.optimization_barrier((mine, own_pair))
    pair = lax.all_gather(own_pair, "tensor", axis=0, tiled=True)
    output, grad_input = pair[:, :width], pair[:, width:].astype(full_type)
    mine = mine.reshape(width, task_width).T.astype(full_type)
    paired = (dp_index == 0) | (dp_index == 4)
    steps = orthogonalize(mine, paired).T.astype(low_type).reshape(dp_count, shard_rows, task_width)
    steps = lax.all_to_all(steps, "dp", split_axis=0, concat_axis=0, tiled=True)
    steps = steps.astype(full_type)

    def rate(rows, columns):
        return MUON_RATE * math.sqrt(max(1.0, rows / columns))

    new_query = w_query - rate(width, head_dim) * steps[0][:, :head_dim]
    new_out = w_out - rate(head_dim, width) * steps[0][:, head_dim:].T
    new_gate_up = w_gate_up - rate(width, hidden) * steps[1:3]
    new_down = w_down - rate(hidden, width) * steps[3].T
    new_kv = w_kv - rate(width, head_dim) * steps[4]
    return (
        output,
        grad_input,
        grad_query,
        grad_kv,
        grad_out,
        grad_gate_up,
        grad_down,
        grad_gains,
        new_query,
        new_kv,
        new_out,
        new_gate_up,
        new_down,
        new_gains,
        new_mom_query,
        new_mom_kv,
        new_mom_out,
        new_mom_gate_up,
        new_mom_down,
        new_mom_gains,
    )


def solution(mesh):
    return jax.shard_map(
        shards,
        mesh=mesh,
        in_specs=(
            P("dp", None),
            P("dp", None),
            P(),
            P("dp", "tensor"),
            P("dp", None),
            P("tensor", "dp"),
            P(None, "dp", "tensor"),
            P("tensor", "dp"),
            P("dp"),
            P("dp", "tensor"),
            P("dp", None),
            P("tensor", "dp"),
            P(None, "dp", "tensor"),
            P("tensor", "dp"),
            P("dp"),
        ),
        out_specs=(
            P("dp", None),
            P("dp", None),
            P("dp", "tensor"),
            P("dp", None),
            P("tensor", "dp"),
            P(None, "dp", "tensor"),
            P("tensor", "dp"),
            P("dp"),
            P("dp", "tensor"),
            P("dp", None),
            P("tensor", "dp"),
            P(None, "dp", "tensor"),
            P("tensor", "dp"),
            P("dp"),
            P("dp", "tensor"),
            P("dp", None),
            P("tensor", "dp"),
            P(None, "dp", "tensor"),
            P("tensor", "dp"),
            P("dp"),
        ),
        check_vma=False,
    )
```
